32 devices in a mesh: group: 2 (over x), tensor: 8 (over z, y), replica: 2 (over core).
Axes of the slice: x: 2, y: 2, z: 4, core: 2. Of those that a mesh axis runs over, the one named last changes fastest.
Arguments:
- hidden_in: bfloat16 [2, 256, 8192], P(None, ('group', 'replica')), parts along dimension 1, may hold values from -6 to 6
- norm_gain: bfloat16 [8192], replicated, may hold values from 0.25 to 1.75
- w_query: bfloat16 [8192, 4096], P(None, 'tensor'), may hold values from -0.0625 to 0.0625
- w_keyval: bfloat16 [8192, 1024], P(None, 'tensor'), may hold values from -0.0625 to 0.0625
- w_out: bfloat16 [4096, 8192], P('tensor'), may hold values from -0.09375 to 0.09375
- cache_kv: bfloat16 [2, 256, 384, 1024], P(None, ('group', 'replica'), None, 'tensor'), parts along dimension 1
- cache_len: int32 [256], P(('group', 'replica')), parts along dimension 0, may hold values from 1 to 384
- prompt_kv: bfloat16 [2, 64, 256, 512], P(None, ('group', 'tensor', 'replica')), parts along dimension 1
- block_count: int32 [64], P('group'), parts along dimension 0, may hold values from 1 to 4
- slot_of: int32 [64], P('group'), parts along dimension 0, may hold values from 0 to 127, as said below
Outputs:
- attended: bfloat16 [2, 256, 8192], P(None, ('group', 'replica'), 'tensor'), parts along dimension 1
The draws below stay inside these ranges and needn't reach their ends.
There are 2 independent parts, one for each index of `group`. The reference program is written for one: setup_inputs(seed, part) draws one part's arguments, and reference() takes and returns one part's arrays. A program takes and returns all parts, laid end to end along the dimension named above; an argument that names none is the same for every part. Nothing has to cross between parts.
Inputs may be any that keep to these rules, and one draw needn't show every extreme that they name: `slot_of`: distinct slots; slot 0 and slot 127 are always taken.
All inputs are finite; a program needn't handle non-finite values.
Results may differ from the reference program's by a relative error of at most 0.012.
The reference program's roundings to bfloat16 on the way count: a program that leaves them out, or rounds other values in their place, can miss the bound.
Values may be sent and summed in bfloat16 or wider, within the bound.
A program may use at most 128 MiB of HBM per device.

```python
import jax
import jax.numpy as jnp
from jax import lax

D = 8192
HEADS = 32
KVH = 4
HD = 128
GROUP = 8
QD = 4
STEPS = 2
CTX = 384
BLOCK = 64
PBLK = 4
PLEN = 256
SLOTS = 128
REQUESTS = 32
CACHE_COLS = 1024
N_TENSOR = 8


def draw_slot_of(key, part):
    key = jax.random.fold_in(key, 5)
    first_key, second_key = jax.random.split(key)
    middle = 1 + jax.random.permutation(first_key, SLOTS - 2)[:REQUESTS - 2]
    chosen = jnp.concatenate([middle.astype(jnp.int32), jnp.array([0, SLOTS - 1], dtype=jnp.int32)])
    return jax.random.permutation(second_key, chosen).astype(jnp.int32)


def draw_cache_kv(key, part):
    key = jax.random.fold_in(key, 7)
    value_key = jax.random.fold_in(key, 0)
    values = jax.random.normal(value_key, (2, SLOTS, CTX, CACHE_COLS), jnp.float32)
    return values.astype(jnp.bfloat16)


def draw_prompt_kv(key, part):
    key = jax.random.fold_in(key, 11)
    value_key = jax.random.fold_in(key, 0)
    values = jax.random.normal(value_key, (2, REQUESTS, PLEN, KVH * HD), jnp.float32)
    return values.astype(jnp.bfloat16)


def set_ends(values, key, smallest, largest):
    index_at = [jax.random.randint(jax.random.fold_in(key, axis), (), 0, length) for axis, length in enumerate(values.shape)]
    longest = values.shape.index(max(values.shape))
    neighbour = index_at[:longest] + [(index_at[longest] + 1) % values.shape[longest]] + index_at[longest + 1:]
    return values.at[tuple(index_at)].set(smallest).at[tuple(neighbour)].set(largest)


def levels(key, dims, cuts, low, top_value):
    def one(axis_at, shards_of):
        heights = jax.random.uniform(jax.random.fold_in(jax.random.fold_in(key, 6), axis_at), (shards_of,), jnp.float32, low / len(cuts), top_value / len(cuts))
        return jnp.repeat(jnp.exp(heights), dims[axis_at] // shards_of).reshape((-1,) + (1,) * (len(dims) - axis_at - 1))

    gain = one(*cuts[0])
    for cut in cuts[1:]:
        gain = gain * one(*cut)
    return gain


def gaussian(own_key, extent, width, limit, cuts=(), kind=jnp.bfloat16):
    entries = jax.random.normal(own_key, extent, jnp.float32) * width
    if len(cuts) > 0:
        entries = levels(own_key, extent, cuts, -0.22, 0.18) * entries
    return jnp.clip(entries, min=-limit, max=limit).astype(kind)


def setup_inputs(seed: int = 0, part: int = 0) -> dict:
    key_of = jax.random.split(jax.random.key(seed), 11)
    part_keys = jax.random.split(jax.random.fold_in(key_of[10], part), 11)
    return {
        "hidden_in": gaussian(part_keys[0], (STEPS, SLOTS, D), 1.0, 6.0, ((1, 2),)),
        "norm_gain": jnp.clip(1.0 + 0.15 * jax.random.normal(key_of[1], (D,), jnp.float32), 0.25, 1.75).astype(jnp.bfloat16),
        "w_query": gaussian(key_of[2], (D, HEADS * HD), D ** -0.5, 0.0625, ((1, 8),)),
        "w_keyval": gaussian(key_of[3], (D, 2 * KVH * HD), D ** -0.5, 0.0625, ((1, 8),)),
        "w_out": gaussian(key_of[4], (HEADS * HD, D), (HEADS * HD) ** -0.5, 0.09375, ((0, 8),)),
        "cache_kv": draw_cache_kv(jax.random.fold_in(jax.random.fold_in(key_of[10], part), 71), part),
        "cache_len": set_ends(jax.random.randint(part_keys[6], (SLOTS,), 1, CTX + 1), jax.random.fold_in(part_keys[6], 1), 1, CTX).astype(jnp.int32),
        "prompt_kv": draw_prompt_kv(jax.random.fold_in(jax.random.fold_in(key_of[10], part), 71), part),
        "block_count": set_ends(jax.random.randint(part_keys[8], (REQUESTS,), 1, PBLK + 1), jax.random.fold_in(part_keys[8], 1), 1, PBLK).astype(jnp.int32),
        "slot_of": draw_slot_of(jax.random.fold_in(jax.random.fold_in(key_of[10], part), 71), part),
    }


EPSILON = 1e-05
THETA = 500000.0
NEGATIVE = -1e+30

def widen(array):
    return array.astype(jnp.float32)

def rotate(values, positions):
    half_dim = values.shape[-1] // 2
    freqs = THETA ** (-2.0 * jnp.arange(half_dim, dtype=jnp.float32) / values.shape[-1])
    angles = positions[..., None].astype(jnp.float32) * freqs
    cosine = jnp.cos(angles)
    sine = jnp.sin(angles)
    first = values[..., :half_dim]
    second = values[..., half_dim:]
    return jnp.concatenate([first * cosine - second * sine, second * cosine + first * sine], -1)

def attend(queries, cache_keys, cache_values, prompt_keys, prompt_values, new_keys, new_values, cache_valid, prompt_valid, own_valid):
    scaling = HD ** (-0.5)
    score_cache = jnp.einsum('jshd,scd->jshc', widen(queries), widen(cache_keys)) * scaling
    score_prompt = jnp.einsum('jshd,spd->jshp', widen(queries), widen(prompt_keys)) * scaling
    score_own = jnp.einsum('jshd,isd->jshi', widen(queries), widen(new_keys)) * scaling
    score_cache = jnp.where(cache_valid[None, :, None, :], score_cache, NEGATIVE)
    score_prompt = jnp.where(prompt_valid[None, :, None, :], score_prompt, NEGATIVE)
    score_own = jnp.where(own_valid[:, None, None, :], score_own, NEGATIVE)
    top = jnp.maximum(jnp.maximum(lax.optimization_barrier(jnp.max(score_cache, -1)), lax.optimization_barrier(jnp.max(score_prompt, -1))), lax.optimization_barrier(jnp.max(score_own, -1)))[..., None]
    exp_cache = jnp.exp(score_cache - top)
    exp_prompt = jnp.exp(score_prompt - top)
    exp_own = jnp.exp(score_own - top)
    summed = (lax.optimization_barrier(jnp.sum(exp_cache, -1)) + lax.optimization_barrier(jnp.sum(exp_prompt, -1)) + lax.optimization_barrier(jnp.sum(exp_own, -1)))[..., None]
    weight_cache = (exp_cache / summed).astype(jnp.bfloat16)
    weight_prompt = (exp_prompt / summed).astype(jnp.bfloat16)
    weight_own = (exp_own / summed).astype(jnp.bfloat16)
    result = jnp.einsum('jshc,scd->jshd', widen(weight_cache), widen(cache_values))
    result = result + jnp.einsum('jshp,spd->jshd', widen(weight_prompt), widen(prompt_values))
    result = result + jnp.einsum('jshi,isd->jshd', widen(weight_own), widen(new_values))
    return result.astype(jnp.bfloat16)

def reference(hidden_in, norm_gain, w_query, w_keyval, w_out, cache_kv, cache_len, prompt_kv, block_count, slot_of):
    hidden = hidden_in.astype(jnp.float32)
    scale = lax.rsqrt(lax.optimization_barrier(jnp.mean(hidden * hidden, -1, keepdims=True)) + EPSILON)
    normed = (hidden * scale * norm_gain.astype(jnp.float32)).astype(jnp.bfloat16)
    flat = normed.reshape(STEPS * SLOTS, D)
    queries = jnp.dot(flat, w_query, preferred_element_type=jnp.float32).reshape(STEPS, SLOTS, HEADS, HD)
    keyval = jnp.dot(flat, w_keyval, preferred_element_type=jnp.float32).astype(jnp.bfloat16)
    keyval = keyval.reshape(STEPS, SLOTS, 2, KVH, HD)
    matches = slot_of[None, :] == jnp.arange(SLOTS, dtype=jnp.int32)[:, None]
    matched = jnp.any(matches, 1)
    request = lax.optimization_barrier(jnp.sum(jnp.where(matches, jnp.arange(REQUESTS, dtype=jnp.int32)[None, :], 0), 1)).astype(jnp.int32)
    prompt_len = (lax.optimization_barrier(jnp.sum(jnp.where(matches, block_count[None, :], 0), 1)) * BLOCK).astype(jnp.int32)
    base_pos = jnp.where(matched, prompt_len, cache_len).astype(jnp.int32)
    positions = base_pos[None, :] + jnp.arange(STEPS, dtype=jnp.int32)[:, None]
    queries = rotate(queries, positions[:, :, None]).astype(jnp.bfloat16)
    new_keys = rotate(widen(keyval[:, :, 0]), positions[:, :, None]).astype(jnp.bfloat16)
    new_values = keyval[:, :, 1]
    prompt_sel = prompt_kv[:, request]
    cache_valid = jnp.logical_not(matched)[:, None] & (jnp.arange(CTX, dtype=jnp.int32)[None, :] < cache_len[:, None])
    prompt_valid = matched[:, None] & (jnp.arange(PLEN, dtype=jnp.int32)[None, :] < prompt_len[:, None])
    own_valid = jnp.arange(STEPS, dtype=jnp.int32)[None, :] <= jnp.arange(STEPS, dtype=jnp.int32)[:, None]

    def one_copy(copy):
        kv_head = copy * QD // GROUP
        cache_part = lax.dynamic_slice_in_dim(cache_kv, copy * HD, HD, 3)
        prompt_part = lax.dynamic_slice_in_dim(prompt_sel, kv_head * HD, HD, 3)
        head_queries = lax.dynamic_slice_in_dim(queries, copy * QD, QD, 2)
        own_keys = lax.dynamic_index_in_dim(new_keys, kv_head, 2, keepdims=False)
        own_values = lax.dynamic_index_in_dim(new_values, kv_head, 2, keepdims=False)
        return attend(head_queries, cache_part[0], cache_part[1], prompt_part[0], prompt_part[1], own_keys, own_values, cache_valid, prompt_valid, own_valid)
    outputs = lax.map(one_copy, jnp.arange(N_TENSOR, dtype=jnp.int32))
    heads_out = jnp.transpose(outputs, (1, 2, 0, 3, 4)).reshape(STEPS * SLOTS, HEADS * HD)
    mixed = jnp.dot(heads_out, w_out, preferred_element_type=jnp.float32)
    return mixed.reshape(STEPS, SLOTS, D).astype(jnp.bfloat16)
```

```python
import functools

import jax
import jax.numpy as jnp
from jax import lax
from jax.experimental import pallas as pl
from jax.experimental.pallas import tpu as pltpu
from jax.sharding import PartitionSpec as P

KVH = 4
HD = 128
GROUP = 8
BLOCK = 64


EPSILON = 1e-05
THETA = 500000.0
NEGATIVE = -1e30
MESH = pl.DeviceIdType.MESH


def out_kernel(size, heads_ref, w_ref, out_ref, wbuf, own, send1, recv1, send2, recv2, wsem, s1s, s1r, s2s, s2r):
    half = size // 2
    rank = lax.axis_index("tensor")
    mine = rank // 2
    side = lax.rem(rank, 2)
    partner = rank + 1 - 2 * side
    width = out_ref.shape[1]
    offsets = [o for o in range(half // 2, half)] + [o for o in range(1, half // 2)] + [0]

    weights = []
    for at, off in enumerate(offsets):
        block = lax.rem(mine + off, half)
        for which, target in enumerate((2 * block + 1 - side, 2 * block + side)):
            columns = pl.ds(pl.multiple_of(target * width, 128), width)
            copy = pltpu.make_async_copy(w_ref.at[:, columns], wbuf.at[at, which], wsem.at[at, which])
            copy.start()
            weights.append(copy)

    barrier = pltpu.get_barrier_semaphore()
    peers = [partner] + [2 * lax.rem(mine + off, half) + side for off in range(1, half)]
    for peer in peers:
        pl.semaphore_signal(barrier, inc=1, device_id={"tensor": peer}, device_id_type=MESH)
    pl.semaphore_wait(barrier, len(peers))

    heads = heads_ref[...]
    first = []
    for at in range(half):
        weights[2 * at].wait()
        send1[at] = jnp.dot(heads, wbuf[at, 0], preferred_element_type=jnp.float32).astype(jnp.bfloat16)
        copy = pltpu.make_async_remote_copy(
            src_ref=send1.at[at], dst_ref=recv1.at[at], send_sem=s1s.at[at], recv_sem=s1r.at[at],
            device_id={"tensor": partner}, device_id_type=MESH)
        copy.start()
        first.append(copy)
    for at in range(half):
        weights[2 * at + 1].wait()
        own[at] = jnp.dot(heads, wbuf[at, 1], preferred_element_type=jnp.float32)
    second = []
    for at, off in enumerate(offsets):
        first[at].wait_recv()
        total = own[at] + recv1[at].astype(jnp.float32)
        if off != 0:
            send2[at] = total.astype(jnp.bfloat16)
            copy = pltpu.make_async_remote_copy(
                src_ref=send2.at[at], dst_ref=recv2.at[at], send_sem=s2s.at[at], recv_sem=s2r.at[at],
                device_id={"tensor": 2 * lax.rem(mine + off, half) + side}, device_id_type=MESH)
            copy.start()
            second.append(copy)
        else:
            own[at] = total
    for at in range(half - 1):
        second[at].wait_recv()
        own[half - 1] += recv2[at].astype(jnp.float32)
    out_ref[...] = own[half - 1].astype(jnp.bfloat16)
    for copy in first + second:
        copy.wait_send()


def project_out(heads, w_out, size):
    rows, depth = heads.shape
    width = w_out.shape[1] // size
    half = size // 2
    return pl.pallas_call(
        functools.partial(out_kernel, size),
        out_shape=jax.ShapeDtypeStruct((rows, width), jnp.bfloat16),
        in_specs=[pl.BlockSpec(memory_space=pltpu.VMEM), pl.BlockSpec(memory_space=pl.ANY)],
        out_specs=pl.BlockSpec(memory_space=pltpu.VMEM),
        scratch_shapes=[
            pltpu.VMEM((half, 2, depth, width), jnp.bfloat16),
            pltpu.VMEM((half, rows, width), jnp.float32),
            pltpu.VMEM((half, rows, width), jnp.bfloat16),
            pltpu.VMEM((half, rows, width), jnp.bfloat16),
            pltpu.VMEM((half - 1, rows, width), jnp.bfloat16),
            pltpu.VMEM((half - 1, rows, width), jnp.bfloat16),
            pltpu.SemaphoreType.DMA((half, 2)),
            pltpu.SemaphoreType.DMA((half,)),
            pltpu.SemaphoreType.DMA((half,)),
            pltpu.SemaphoreType.DMA((half - 1,)),
            pltpu.SemaphoreType.DMA((half - 1,)),
        ],
        compiler_params=pltpu.CompilerParams(collective_id=1, has_side_effects=True, vmem_limit_bytes=40 * 2**20),
    )(heads, w_out)


def rotate(values, positions):
    half_dim = values.shape[-1] // 2
    freqs = THETA ** (-2.0 * jnp.arange(half_dim, dtype=jnp.float32) / values.shape[-1])
    angles = positions[..., None].astype(jnp.float32) * freqs
    cosine = jnp.cos(angles)
    sine = jnp.sin(angles)
    first = values[..., :half_dim]
    second = values[..., half_dim:]
    return jnp.concatenate([first * cosine - second * sine, second * cosine + first * sine], -1)


def attend(
    queries,
    cache_keys,
    cache_values,
    prompt_keys,
    prompt_values,
    new_keys,
    new_values,
    cache_valid,
    prompt_valid,
    own_valid,
):
    scaling = HD ** (-0.5)
    score_cache = (
        jnp.einsum("jshd,scd->jshc", queries, cache_keys, preferred_element_type=jnp.float32)
        * scaling
    )
    score_prompt = (
        jnp.einsum("jshd,spd->jshp", queries, prompt_keys, preferred_element_type=jnp.float32)
        * scaling
    )
    score_own = (
        jnp.einsum("jshd,isd->jshi", queries, new_keys, preferred_element_type=jnp.float32)
        * scaling
    )
    score_cache = jnp.where(cache_valid[None, :, None, :], score_cache, NEGATIVE)
    score_prompt = jnp.where(prompt_valid[None, :, None, :], score_prompt, NEGATIVE)
    score_own = jnp.where(own_valid[:, None, None, :], score_own, NEGATIVE)
    top = jnp.maximum(
        jnp.maximum(jnp.max(score_cache, -1), jnp.max(score_prompt, -1)), jnp.max(score_own, -1)
    )[..., None]
    exp_cache = jnp.exp(score_cache - top)
    exp_prompt = jnp.exp(score_prompt - top)
    exp_own = jnp.exp(score_own - top)
    summed = (jnp.sum(exp_cache, -1) + jnp.sum(exp_prompt, -1) + jnp.sum(exp_own, -1))[..., None]
    weight_cache = (exp_cache / summed).astype(jnp.bfloat16)
    weight_prompt = (exp_prompt / summed).astype(jnp.bfloat16)
    weight_own = (exp_own / summed).astype(jnp.bfloat16)
    result = jnp.einsum(
        "jshc,scd->jshd", weight_cache, cache_values, preferred_element_type=jnp.float32
    )
    result = result + jnp.einsum(
        "jshp,spd->jshd", weight_prompt, prompt_values, preferred_element_type=jnp.float32
    )
    result = result + jnp.einsum(
        "jshi,isd->jshd", weight_own, new_values, preferred_element_type=jnp.float32
    )
    return result.astype(jnp.bfloat16)


def local(
    hidden_in,
    norm_gain,
    w_query,
    w_keyval,
    w_out,
    cache_kv,
    cache_len,
    prompt_kv,
    block_count,
    slot_of,
):
    tensor_size = lax.axis_size("tensor")
    replica_size = lax.axis_size("replica")
    tensor_rank = lax.axis_index("tensor")
    replica_rank = lax.axis_index("replica")
    step_count, row_count, model_width = hidden_in.shape
    local_heads = w_query.shape[1] // HD
    kv_head = tensor_rank * local_heads // GROUP
    per_device = prompt_kv.shape[1]
    prompt_cap = prompt_kv.shape[2]
    capacity = cache_kv.shape[2]
    hidden = hidden_in.astype(jnp.float32)
    scale = lax.rsqrt(jnp.mean(hidden * hidden, -1, keepdims=True) + EPSILON)
    normed = (hidden * scale * norm_gain.astype(jnp.float32)).astype(jnp.bfloat16)
    flat = normed.reshape(step_count * row_count, model_width)
    queries = jnp.dot(flat, w_query, preferred_element_type=jnp.float32).reshape(
        step_count, row_count, local_heads, HD
    )
    keyval_part = jnp.dot(flat, w_keyval, preferred_element_type=jnp.float32).astype(jnp.bfloat16)
    keyval_part = keyval_part.reshape(step_count, row_count, -1)
    keyval = lax.all_gather(keyval_part, "tensor", axis=2, tiled=True).reshape(
        step_count, row_count, 2, KVH, HD
    )
    own_pair = lax.dynamic_index_in_dim(keyval, kv_head, 3, keepdims=False)
    slot_ids = replica_rank * row_count + jnp.arange(row_count, dtype=jnp.int32)
    matches = slot_of[None, :] == slot_ids[:, None]
    matched = jnp.any(matches, 1)
    request_count = slot_of.shape[0]
    request = jnp.sum(jnp.where(matches, jnp.arange(request_count, dtype=jnp.int32)[None, :], 0), 1)
    prompt_len = jnp.sum(jnp.where(matches, block_count[None, :], 0), 1) * BLOCK
    base_pos = jnp.where(matched, prompt_len, cache_len)
    positions = base_pos[None, :] + jnp.arange(step_count, dtype=jnp.int32)[:, None]
    queries = rotate(queries, positions[:, :, None]).astype(jnp.bfloat16)
    new_keys = rotate(own_pair[:, :, 0].astype(jnp.float32), positions).astype(jnp.bfloat16)
    new_values = own_pair[:, :, 1]
    everything = lax.all_gather(prompt_kv, "tensor", axis=1, tiled=True)
    own_prompts = lax.dynamic_slice_in_dim(everything, kv_head * HD, HD, 3)
    paired = lax.all_gather(own_prompts, "replica", axis=1, tiled=True)
    sender = request // per_device
    within = request % per_device
    sender_tensor = sender // replica_size
    sender_replica = sender % replica_size
    position = (sender_replica * tensor_size + sender_tensor) * per_device + within
    chosen = jnp.take(paired, position, axis=1)
    cache_valid = jnp.logical_not(matched)[:, None] & (
        jnp.arange(capacity, dtype=jnp.int32)[None, :] < cache_len[:, None]
    )
    prompt_valid = matched[:, None] & (
        jnp.arange(prompt_cap, dtype=jnp.int32)[None, :] < prompt_len[:, None]
    )
    own_valid = (
        jnp.arange(step_count, dtype=jnp.int32)[None, :]
        <= jnp.arange(step_count, dtype=jnp.int32)[:, None]
    )
    heads_out = attend(
        queries,
        cache_kv[0],
        cache_kv[1],
        chosen[0],
        chosen[1],
        new_keys,
        new_values,
        cache_valid,
        prompt_valid,
        own_valid,
    )
    heads_flat = heads_out.reshape(step_count * row_count, local_heads * HD)
    mixed = project_out(heads_flat, w_out, tensor_size)
    return mixed.reshape(step_count, row_count, -1)


def solution(mesh):
    in_specs = (
        P(None, ("group", "replica"), None),
        P(),
        P(None, "tensor"),
        P(None, "tensor"),
        P("tensor", None),
        P(None, ("group", "replica"), None, "tensor"),
        P(("group", "replica")),
        P(None, ("group", "tensor", "replica"), None, None),
        P("group"),
        P("group"),
    )
    out_specs = P(None, ("group", "replica"), "tensor")
    return jax.shard_map(local, mesh=mesh, in_specs=in_specs, out_specs=out_specs, check_vma=False)
```

```python
import functools

import jax
import jax.numpy as jnp
from jax import lax
from jax.experimental import pallas as pl
from jax.experimental.pallas import tpu as pltpu
from jax.sharding import PartitionSpec as P

KVH = 4
HD = 128
GROUP = 8
BLOCK = 64


EPSILON = 1e-05
THETA = 500000.0
NEGATIVE = -1e30
MESH = pl.DeviceIdType.MESH


def out_kernel(size, heads_ref, w_ref, out_ref, wbuf, own, send1, recv1, send2, recv2, wsem, s1s, s1r, s2s, s2r):
    half = size // 2
    rank = lax.axis_index("tensor")
    mine = rank // 2
    side = lax.rem(rank, 2)
    partner = rank + 1 - 2 * side
    width = out_ref.shape[1]
    offsets = [o for o in range(half // 2, half)] + [o for o in range(1, half // 2)] + [0]

    weights = []
    for at, off in enumerate(offsets):
        block = lax.rem(mine + off, half)
        for which, target in enumerate((2 * block + 1 - side, 2 * block + side)):
            columns = pl.ds(pl.multiple_of(target * width, 128), width)
            copy = pltpu.make_async_copy(w_ref.at[:, columns], wbuf.at[at, which], wsem.at[at, which])
            copy.start()
            weights.append(copy)

    barrier = pltpu.get_barrier_semaphore()
    peers = [partner] + [2 * lax.rem(mine + off, half) + side for off in range(1, half)]
    for peer in peers:
        pl.semaphore_signal(barrier, inc=1, device_id={"tensor": peer}, device_id_type=MESH)
    pl.semaphore_wait(barrier, len(peers))

    heads = heads_ref[...]
    first = []
    for at in range(half):
        weights[2 * at].wait()
        send1[at] = jnp.dot(heads, wbuf[at, 0], preferred_element_type=jnp.float32).astype(jnp.bfloat16)
        copy = pltpu.make_async_remote_copy(
            src_ref=send1.at[at], dst_ref=recv1.at[at], send_sem=s1s.at[at], recv_sem=s1r.at[at],
            device_id={"tensor": partner}, device_id_type=MESH)
        copy.start()
        first.append(copy)
    for at in range(half):
        weights[2 * at + 1].wait()
        own[at] = jnp.dot(heads, wbuf[at, 1], preferred_element_type=jnp.float32)
    second = []
    for at, off in enumerate(offsets):
        first[at].wait_recv()
        total = own[at] + recv1[at].astype(jnp.float32)
        if off != 0:
            send2[at] = total.astype(jnp.bfloat16)
            copy = pltpu.make_async_remote_copy(
                src_ref=send2.at[at], dst_ref=recv2.at[at], send_sem=s2s.at[at], recv_sem=s2r.at[at],
                device_id={"tensor": 2 * lax.rem(mine + off, half) + side}, device_id_type=MESH)
            copy.start()
            second.append(copy)
        else:
            own[at] = total
    for at in range(half - 1):
        second[at].wait_recv()
        own[half - 1] += recv2[at].astype(jnp.float32)
    out_ref[...] = own[half - 1].astype(jnp.bfloat16)
    for copy in first + second:
        copy.wait_send()


def project_out(heads, w_out, size):
    rows, depth = heads.shape
    width = w_out.shape[1] // size
    half = size // 2
    return pl.pallas_call(
        functools.partial(out_kernel, size),
        out_shape=jax.ShapeDtypeStruct((rows, width), jnp.bfloat16),
        in_specs=[pl.BlockSpec(memory_space=pltpu.VMEM), pl.BlockSpec(memory_space=pl.ANY)],
        out_specs=pl.BlockSpec(memory_space=pltpu.VMEM),
        scratch_shapes=[
            pltpu.VMEM((half, 2, depth, width), jnp.bfloat16),
            pltpu.VMEM((half, rows, width), jnp.float32),
            pltpu.VMEM((half, rows, width), jnp.bfloat16),
            pltpu.VMEM((half, rows, width), jnp.bfloat16),
            pltpu.VMEM((half - 1, rows, width), jnp.bfloat16),
            pltpu.VMEM((half - 1, rows, width), jnp.bfloat16),
            pltpu.SemaphoreType.DMA((half, 2)),
            pltpu.SemaphoreType.DMA((half,)),
            pltpu.SemaphoreType.DMA((half,)),
            pltpu.SemaphoreType.DMA((half - 1,)),
            pltpu.SemaphoreType.DMA((half - 1,)),
        ],
        compiler_params=pltpu.CompilerParams(collective_id=1, has_side_effects=True, vmem_limit_bytes=40 * 2**20),
    )(heads, w_out)

def attend(query, keys, values, length, own_keys, own_values, local_heads):
    scaling = HD ** (-0.5)
    score = lax.dot_general(
        query.astype(jnp.bfloat16), keys, (((1,), (1,)), ((), ())), preferred_element_type=jnp.float32
    ) * scaling
    score = jnp.where(lax.broadcasted_iota(jnp.int32, score.shape, 1) < length, score, NEGATIVE)
    step_of = lax.broadcasted_iota(jnp.int32, (query.shape[0], 1), 0) // local_heads
    own = []
    for step, key in enumerate(own_keys):
        one = jnp.sum(query * key, axis=1, keepdims=True) * scaling
        own.append(jnp.where(step_of >= step, one, NEGATIVE))
    top = jnp.max(score, axis=1, keepdims=True)
    for one in own:
        top = jnp.maximum(top, one)
    score = jnp.exp(score - top)
    own = [jnp.exp(one - top) for one in own]
    summed = jnp.sum(score, axis=1, keepdims=True)
    for one in own:
        summed = summed + one
    inverse = 1.0 / summed
    result = jnp.dot((score * inverse).astype(jnp.bfloat16), values, preferred_element_type=jnp.float32)
    for one, value in zip(own, own_values):
        result = result + (one * inverse).astype(jnp.bfloat16).astype(jnp.float32) * value
    return result


def attend_kernel(
    size, length_ref, plength_ref, local_ref, request_ref, matched_ref,
    query_ref, part_ref, cosine_ref, sine_ref, cache_ref, prompt_ref, heads_ref,
    cache, prompts, parts, new_keys, new_values, cache_out, prompt_out,
    csem, lsem, p1s, p1r, p2s, p2r, p3s, p3r, ks, kr,
):
    slots, head_rows, _ = query_ref.shape
    steps = new_keys.shape[0]
    local_heads = head_rows // steps
    kv_heads = prompt_ref.shape[3] // HD
    per_device = prompt_ref.shape[1]
    share = size // kv_heads
    pieces = parts.shape[1]
    rank = lax.axis_index("tensor")
    copy_of = lax.axis_index("replica")
    head = rank // share
    side = lax.rem(rank, share)
    offsets = [0] + list(range(kv_heads // 2, kv_heads)) + list(range(1, kv_heads // 2))
    chunk = 8

    loads = []
    chunks = slots // chunk
    for at in range(chunks):
        rows = pl.ds(at * chunk, chunk)
        copy = pltpu.make_async_copy(cache_ref.at[:, rows], cache.at[:, rows], csem.at[at])
        copy.start()
        loads.append(copy)

    barrier = pltpu.get_barrier_semaphore()
    for off in range(1, size):
        pl.semaphore_signal(barrier, inc=1, device_id={"tensor": lax.rem(rank + off, size)}, device_id_type=MESH)
    pl.semaphore_signal(barrier, inc=1, device_id={"replica": 1 - copy_of}, device_id_type=MESH)
    pl.semaphore_wait(barrier, size)

    column = rank // pieces
    kind = column // kv_heads
    piece = lax.rem(rank, pieces)
    part_copies = []
    for at in range(share):
        target = lax.rem(column, kv_heads) * share + at
        remote = pltpu.make_async_remote_copy(
            src_ref=part_ref, dst_ref=parts.at[kind, piece], send_sem=ks.at[at], recv_sem=kr.at[kind, piece],
            device_id={"tensor": target}, device_id_type=MESH)
        part_copies.append((target, remote))

        @pl.when(target != rank)
        def _(remote=remote):
            remote.start()

        @pl.when(target == rank)
        def _():
            pltpu.make_async_copy(part_ref, parts.at[kind, piece], kr.at[kind, piece]).start()

    def slot_of(plane, side_at, replica_at):
        return (plane * share + side_at) * 2 + replica_at

    def arrive(slot, sem):
        pltpu.make_async_copy(prompts.at[slot], prompts.at[slot], sem).wait()

    sent = []

    def send(src, slot, send_sem, recv_sem, device):
        copy = pltpu.make_async_remote_copy(
            src_ref=src, dst_ref=prompts.at[slot], send_sem=send_sem, recv_sem=recv_sem,
            device_id=device, device_id_type=MESH)
        copy.start()
        sent.append(copy)

    def plane_of(at):
        return lax.rem(head + kv_heads - offsets[at], kv_heads)

    def slab(which):
        return prompt_ref.at[:, :, :, pl.ds(pl.multiple_of(which * HD, HD), HD)]

    mine = slot_of(head, side, copy_of)
    for at in range(1, kv_heads):
        target = lax.rem(head + offsets[at], kv_heads)
        send(slab(target), mine, p1s.at[at], p1r.at[at], {"tensor": target * share + side})
    keep = pltpu.make_async_copy(slab(head), prompts.at[mine], lsem)
    keep.start()

    def spread(at, src, slot):
        for other in range(1, share):
            target = head * share + lax.rem(side + other, share)
            send(src, slot, p2s.at[other, at], p2r.at[other, at], {"tensor": target})
        send(src, slot, p3s.at[0, at], p3r.at[0, at], {"replica": 1 - copy_of})

    def pass_on(at):
        for other in range(1, share):
            slot = slot_of(plane_of(at), lax.rem(side + share - other, share), copy_of)
            arrive(slot, p2r.at[other, at])
            send(prompts.at[slot], slot, p3s.at[other, at], p3r.at[other, at], {"replica": 1 - copy_of})

    spread(0, slab(head), mine)

    for which in range(2):
        for at in range(pieces):
            pltpu.make_async_copy(parts.at[which, at], parts.at[which, at], kr.at[which, at]).wait()
    joined = [
        jnp.concatenate([parts[which, at] for at in range(pieces)], axis=1).astype(jnp.float32)
        for which in range(2)
    ]
    turned = joined[0] * cosine_ref[...] + pltpu.roll(joined[0], HD // 2, 1) * sine_ref[...]
    turned = turned.astype(jnp.bfloat16).astype(jnp.float32)
    for step in range(steps):
        new_keys[step] = turned[step * slots:(step + 1) * slots]
        new_values[step] = joined[1][step * slots:(step + 1) * slots]

    def own_of(slot):
        row = pl.ds(slot, 1)
        return [new_keys[i, row, :] for i in range(steps)], [new_values[i, row, :] for i in range(steps)]

    def cache_chunk(at, carry):
        for inner in range(chunk):
            slot = at * chunk + inner
            keys, values = own_of(slot)
            cache_out[slot] = attend(
                query_ref[slot], cache[0, slot], cache[1, slot], length_ref[slot], keys, values, local_heads)
        return carry

    groups = kv_heads
    each = chunks // groups
    for group in range(groups):
        if group + 1 < kv_heads:
            slot = slot_of(plane_of(group + 1), side, copy_of)
            arrive(slot, p1r.at[group + 1])
            spread(group + 1, prompts.at[slot], slot)
        pass_on(group)
        for at in range(group * each, (group + 1) * each):
            loads[at].wait()
        lax.fori_loop(group * each, (group + 1) * each, cache_chunk, 0)

    keep.wait()
    per_plane = share * 2 * per_device
    batch = min(8, per_plane)
    for group in range(kv_heads):
        plane = plane_of(group)
        for other in range(share):
            arrive(slot_of(plane, lax.rem(side + share - other, share), 1 - copy_of), p3r.at[other, group])

        def prompt_chunk(at, carry, plane=plane):
            for inner in range(batch):
                sender = plane * (share * 2) + at * (batch // per_device) + inner // per_device
                within = inner % per_device
                request = sender * per_device + within
                slot = local_ref[request]
                keys, values = own_of(slot)
                prompt_out[request] = attend(
                    query_ref[slot], prompts[sender, 0, within], prompts[sender, 1, within],
                    plength_ref[request], keys, values, local_heads)
            return carry

        lax.fori_loop(0, per_plane // batch, prompt_chunk, 0)

    def choose(slot, carry):
        cache_out[slot] = jnp.where(matched_ref[slot] > 0, prompt_out[request_ref[slot]], cache_out[slot])
        return carry

    lax.fori_loop(0, slots, choose, 0)
    for step in range(steps):
        for at in range(local_heads):
            heads_ref[pl.ds(step * slots, slots), pl.ds(at * HD, HD)] = cache_out[
                :, step * local_heads + at, :].astype(jnp.bfloat16)

    for copy in sent:
        copy.wait_send()
    for target, copy in part_copies:
        @pl.when(target != rank)
        def _(copy=copy):
            copy.wait_send()


def attention(lengths, plengths, local_slot, request, matched, queries, part, cosine, sine, cache_kv, prompt_kv, size):
    slots, head_rows, _ = queries.shape
    rows, width = part.shape
    steps = rows // slots
    kv_heads = prompt_kv.shape[3] // HD
    share = size // kv_heads
    requests = plengths.shape[0]
    senders = requests // prompt_kv.shape[1]
    smem = pl.BlockSpec(memory_space=pltpu.SMEM)
    vmem = pl.BlockSpec(memory_space=pltpu.VMEM)
    hbm = pl.BlockSpec(memory_space=pl.ANY)
    dma = pltpu.SemaphoreType.DMA
    return pl.pallas_call(
        functools.partial(attend_kernel, size),
        out_shape=jax.ShapeDtypeStruct((rows, head_rows // steps * HD), jnp.bfloat16),
        in_specs=[smem] * 5 + [vmem] * 4 + [hbm] * 2,
        out_specs=vmem,
        scratch_shapes=[
            pltpu.VMEM(cache_kv.shape, jnp.bfloat16),
            pltpu.VMEM((senders, 2, prompt_kv.shape[1], prompt_kv.shape[2], HD), jnp.bfloat16),
            pltpu.VMEM((2, HD // width, rows, width), jnp.bfloat16),
            pltpu.VMEM((steps, slots, HD), jnp.float32),
            pltpu.VMEM((steps, slots, HD), jnp.float32),
            pltpu.VMEM(queries.shape, jnp.float32),
            pltpu.VMEM((requests, head_rows, HD), jnp.float32),
            dma((slots // 8,)),
            dma,
            dma((kv_heads,)), dma((kv_heads,)),
            dma((share, kv_heads)), dma((share, kv_heads)),
            dma((share, kv_heads)), dma((share, kv_heads)),
            dma((share,)), dma((2, HD // width)),
        ],
        compiler_params=pltpu.CompilerParams(collective_id=2, has_side_effects=True, vmem_limit_bytes=48 * 2**20),
    )(lengths, plengths, local_slot, request, matched, queries, part, cosine, sine, cache_kv, prompt_kv)

def local(
    hidden_in,
    norm_gain,
    w_query,
    w_keyval,
    w_out,
    cache_kv,
    cache_len,
    prompt_kv,
    block_count,
    slot_of,
):
    tensor_size = lax.axis_size("tensor")
    replica_rank = lax.axis_index("replica")
    step_count, row_count, model_width = hidden_in.shape
    local_heads = w_query.shape[1] // HD
    hidden = hidden_in.astype(jnp.float32)
    scale = lax.rsqrt(jnp.mean(hidden * hidden, -1, keepdims=True) + EPSILON)
    normed = (hidden * scale * norm_gain.astype(jnp.float32)).astype(jnp.bfloat16)
    flat = normed.reshape(step_count * row_count, model_width)
    queries = jnp.dot(flat, w_query, preferred_element_type=jnp.float32).reshape(
        step_count, row_count, local_heads, HD
    )
    keyval_part = jnp.dot(flat, w_keyval, preferred_element_type=jnp.float32).astype(jnp.bfloat16)
    slot_ids = replica_rank * row_count + jnp.arange(row_count, dtype=jnp.int32)
    matches = slot_of[None, :] == slot_ids[:, None]
    matched = jnp.any(matches, 1)
    request_count = slot_of.shape[0]
    request = jnp.sum(jnp.where(matches, jnp.arange(request_count, dtype=jnp.int32)[None, :], 0), 1)
    prompt_len = jnp.sum(jnp.where(matches, block_count[None, :], 0), 1) * BLOCK
    base_pos = jnp.where(matched, prompt_len, cache_len)
    positions = base_pos[None, :] + jnp.arange(step_count, dtype=jnp.int32)[:, None]
    half_dim = HD // 2
    freqs = THETA ** (-2.0 * jnp.arange(half_dim, dtype=jnp.float32) / HD)
    angles = positions[..., None].astype(jnp.float32) * freqs
    cosine = jnp.cos(angles)
    sine = jnp.sin(angles)
    cosine = jnp.concatenate([cosine, cosine], -1)
    sine = jnp.concatenate([-sine, sine], -1)
    swapped = jnp.concatenate([queries[..., half_dim:], queries[..., :half_dim]], -1)
    queries = queries * cosine[:, :, None] + swapped * sine[:, :, None]
    queries = queries.astype(jnp.bfloat16).astype(jnp.float32)
    queries = queries.transpose(1, 0, 2, 3).reshape(row_count, step_count * local_heads, HD)
    local_slot = jnp.clip(slot_of - replica_rank * row_count, 0, row_count - 1)
    heads_flat = attention(
        cache_len,
        block_count * BLOCK,
        local_slot,
        request,
        matched.astype(jnp.int32),
        queries,
        keyval_part,
        cosine.reshape(step_count * row_count, HD),
        sine.reshape(step_count * row_count, HD),
        cache_kv,
        prompt_kv,
        tensor_size,
    )
    mixed = project_out(heads_flat, w_out, tensor_size)
    return mixed.reshape(step_count, row_count, -1)


def solution(mesh):
    in_specs = (
        P(None, ("group", "replica"), None),
        P(),
        P(None, "tensor"),
        P(None, "tensor"),
        P("tensor", None),
        P(None, ("group", "replica"), None, "tensor"),
        P(("group", "replica")),
        P(None, ("group", "tensor", "replica"), None, None),
        P("group"),
        P("group"),
    )
    out_specs = P(None, ("group", "replica"), "tensor")
    return jax.shard_map(local, mesh=mesh, in_specs=in_specs, out_specs=out_specs, check_vma=False)
```

```python
import functools

import jax
import jax.numpy as jnp
from jax import lax
from jax.experimental import pallas as pl
from jax.experimental.pallas import tpu as pltpu
from jax.sharding import PartitionSpec as P

KVH = 4
HD = 128
GROUP = 8
BLOCK = 64


EPSILON = 1e-05
THETA = 500000.0
NEGATIVE = -1e30
MESH = pl.DeviceIdType.MESH


def load_out(size, w_ref, wbuf, wsem, width):
    half = size // 2
    rank = lax.axis_index("tensor")
    mine = rank // 2
    side = lax.rem(rank, 2)
    offsets = [o for o in range(half // 2, half)] + [o for o in range(1, half // 2)] + [0]

    weights = []
    for at, off in enumerate(offsets):
        block = lax.rem(mine + off, half)
        for which, target in enumerate((2 * block + 1 - side, 2 * block + side)):
            columns = pl.ds(pl.multiple_of(target * width, 128), width)
            copy = pltpu.make_async_copy(w_ref.at[:, columns], wbuf.at[at, which], wsem.at[at, which])
            copy.start()
            weights.append(copy)
    return weights


def project_out(size, weights, heads_ref, out_ref, wbuf, own, send1, recv1, send2, recv2, s1s, s1r, s2s, s2r):
    half = size // 2
    rank = lax.axis_index("tensor")
    mine = rank // 2
    side = lax.rem(rank, 2)
    partner = rank + 1 - 2 * side
    offsets = [o for o in range(half // 2, half)] + [o for o in range(1, half // 2)] + [0]

    heads = heads_ref[...]
    first = []
    for at in range(half):
        weights[2 * at].wait()
        send1[at] = jnp.dot(heads, wbuf[at, 0], preferred_element_type=jnp.float32).astype(jnp.bfloat16)
        copy = pltpu.make_async_remote_copy(
            src_ref=send1.at[at], dst_ref=recv1.at[at], send_sem=s1s.at[at], recv_sem=s1r.at[at],
            device_id={"tensor": partner}, device_id_type=MESH)
        copy.start()
        first.append(copy)
    for at in range(half):
        weights[2 * at + 1].wait()
        own[at] = jnp.dot(heads, wbuf[at, 1], preferred_element_type=jnp.float32)
    second = []
    for at, off in enumerate(offsets):
        first[at].wait_recv()
        total = own[at] + recv1[at].astype(jnp.float32)
        if off != 0:
            send2[at] = total.astype(jnp.bfloat16)
            copy = pltpu.make_async_remote_copy(
                src_ref=send2.at[at], dst_ref=recv2.at[at], send_sem=s2s.at[at], recv_sem=s2r.at[at],
                device_id={"tensor": 2 * lax.rem(mine + off, half) + side}, device_id_type=MESH)
            copy.start()
            second.append(copy)
        else:
            own[at] = total
    for at in range(half - 1):
        second[at].wait_recv()
        own[half - 1] += recv2[at].astype(jnp.float32)
    out_ref[...] = own[half - 1].astype(jnp.bfloat16)
    for copy in first + second:
        copy.wait_send()


def attend(query, keys, values, length, own_keys, own_values, local_heads):
    scaling = HD ** (-0.5)
    score = lax.dot_general(
        query.astype(jnp.bfloat16), keys, (((1,), (1,)), ((), ())), preferred_element_type=jnp.float32
    ) * scaling
    score = jnp.where(lax.broadcasted_iota(jnp.int32, score.shape, 1) < length, score, NEGATIVE)
    step_of = lax.broadcasted_iota(jnp.int32, (query.shape[0], 1), 0) // local_heads
    own = []
    for step, key in enumerate(own_keys):
        one = jnp.sum(query * key, axis=1, keepdims=True) * scaling
        own.append(jnp.where(step_of >= step, one, NEGATIVE))
    top = jnp.max(score, axis=1, keepdims=True)
    for one in own:
        top = jnp.maximum(top, one)
    score = jnp.exp(score - top)
    own = [jnp.exp(one - top) for one in own]
    summed = jnp.sum(score, axis=1, keepdims=True)
    for one in own:
        summed = summed + one
    inverse = 1.0 / summed
    result = jnp.dot((score * inverse).astype(jnp.bfloat16), values, preferred_element_type=jnp.float32)
    for one, value in zip(own, own_values):
        result = result + (one * inverse).astype(jnp.bfloat16).astype(jnp.float32) * value
    return result


def whole_kernel(
    size, length_ref, plength_ref, local_ref, request_ref, matched_ref,
    gain_ref, cosine_ref, sine_ref, hidden_ref, wq_ref, wkv_ref, cache_ref, prompt_ref, w_ref, out_ref,
    normed, wq, wkv, query_sum, part_sum, part_ref, query_ref, heads_ref,
    cache, prompts, parts, new_keys, new_values, cache_out, prompt_out,
    wbuf, own_sum, send1, recv1, send2, recv2,
    hsem, qsem, vsem, csem, lsem, p1s, p1r, p2s, p2r, p3s, p3r, ks, kr, wsem, s1s, s1r, s2s, s2r,
):
    slots, head_rows, _ = query_ref.shape
    depth = wq.shape[0] // qsem.shape[0]
    steps = new_keys.shape[0]
    local_heads = head_rows // steps
    kv_heads = prompt_ref.shape[3] // HD
    per_device = prompt_ref.shape[1]
    share = size // kv_heads
    pieces = parts.shape[1]
    rank = lax.axis_index("tensor")
    copy_of = lax.axis_index("replica")
    head = rank // share
    side = lax.rem(rank, share)
    offsets = [0] + list(range(kv_heads // 2, kv_heads)) + list(range(1, kv_heads // 2))
    chunk = 8

    hidden_loads = []
    for step in range(steps):
        copy = pltpu.make_async_copy(hidden_ref.at[step], normed.at[pl.ds(step * slots, slots)], hsem.at[step])
        copy.start()
        hidden_loads.append(copy)

    def weight_loads(at):
        deep = pl.ds(pl.multiple_of(at * depth, depth), depth)
        return (
            pltpu.make_async_copy(wq_ref.at[deep], wq.at[deep], qsem.at[at]),
            pltpu.make_async_copy(wkv_ref.at[deep], wkv.at[deep], vsem.at[at]),
        )

    for at in range(qsem.shape[0]):
        for copy in weight_loads(at):
            copy.start()

    barrier = pltpu.get_barrier_semaphore()
    for off in range(1, size):
        pl.semaphore_signal(barrier, inc=1, device_id={"tensor": lax.rem(rank + off, size)}, device_id_type=MESH)
    pl.semaphore_signal(barrier, inc=1, device_id={"replica": 1 - copy_of}, device_id_type=MESH)
    pl.semaphore_wait(barrier, size)

    def slot_of(plane, side_at, replica_at):
        return (plane * share + side_at) * 2 + replica_at

    def arrive(slot, sem):
        pltpu.make_async_copy(prompts.at[slot], prompts.at[slot], sem).wait()

    sent = []

    def send(src, slot, send_sem, recv_sem, device):
        copy = pltpu.make_async_remote_copy(
            src_ref=src, dst_ref=prompts.at[slot], send_sem=send_sem, recv_sem=recv_sem,
            device_id=device, device_id_type=MESH)
        copy.start()
        sent.append(copy)

    def plane_of(at):
        return lax.rem(head + kv_heads - offsets[at], kv_heads)

    def slab(which):
        return prompt_ref.at[:, :, :, pl.ds(pl.multiple_of(which * HD, HD), HD)]

    mine = slot_of(head, side, copy_of)
    for at in range(1, kv_heads):
        target = lax.rem(head + offsets[at], kv_heads)
        send(slab(target), mine, p1s.at[at], p1r.at[at], {"tensor": target * share + side})
    keep = pltpu.make_async_copy(slab(head), prompts.at[mine], lsem)
    keep.start()

    def spread(at, src, slot):
        for other in range(1, share):
            target = head * share + lax.rem(side + other, share)
            send(src, slot, p2s.at[other, at], p2r.at[other, at], {"tensor": target})
        send(src, slot, p3s.at[0, at], p3r.at[0, at], {"replica": 1 - copy_of})

    def pass_on(at):
        for other in range(1, share):
            slot = slot_of(plane_of(at), lax.rem(side + share - other, share), copy_of)
            arrive(slot, p2r.at[other, at])
            send(prompts.at[slot], slot, p3s.at[other, at], p3r.at[other, at], {"replica": 1 - copy_of})

    spread(0, slab(head), mine)

    loads = []
    chunks = slots // chunk
    for at in range(chunks):
        rows = pl.ds(at * chunk, chunk)
        copy = pltpu.make_async_copy(cache_ref.at[:, rows], cache.at[:, rows], csem.at[at])
        copy.start()
        loads.append(copy)
    weights = load_out(size, w_ref, wbuf, wsem, out_ref.shape[1])

    for copy in hidden_loads:
        copy.wait()

    def normalize(at, carry):
        rows = pl.ds(pl.multiple_of(at * 16, 16), 16)
        hidden = normed[rows, :].astype(jnp.float32)
        scale = lax.rsqrt(jnp.mean(hidden * hidden, axis=1, keepdims=True) + EPSILON)
        normed[rows, :] = (hidden * scale * gain_ref[...]).astype(jnp.bfloat16)
        return carry

    lax.fori_loop(0, normed.shape[0] // 16, normalize, 0)
    query_sum[...] = jnp.zeros_like(query_sum)
    part_sum[...] = jnp.zeros_like(part_sum)

    def project_in(at, carry):
        for copy in weight_loads(at):
            copy.wait()
        deep = pl.ds(pl.multiple_of(at * depth, depth), depth)
        part = normed[:, deep]
        query_sum[...] += jnp.dot(part, wq[deep, :], preferred_element_type=jnp.float32)
        part_sum[...] += jnp.dot(part, wkv[deep, :], preferred_element_type=jnp.float32)
        return carry

    lax.fori_loop(0, qsem.shape[0], project_in, 0)
    part_ref[...] = part_sum[...].astype(jnp.bfloat16)

    column = rank // pieces
    kind = column // kv_heads
    piece = lax.rem(rank, pieces)
    part_copies = []
    for at in range(share):
        target = lax.rem(column, kv_heads) * share + at
        remote = pltpu.make_async_remote_copy(
            src_ref=part_ref, dst_ref=parts.at[kind, piece], send_sem=ks.at[at], recv_sem=kr.at[kind, piece],
            device_id={"tensor": target}, device_id_type=MESH)
        part_copies.append((target, remote))

        @pl.when(target != rank)
        def _(remote=remote):
            remote.start()

        @pl.when(target == rank)
        def _():
            pltpu.make_async_copy(part_ref, parts.at[kind, piece], kr.at[kind, piece]).start()

    def turn(values):
        turned = values * cosine_ref[rows_of, :] + pltpu.roll(values, HD // 2, 1) * sine_ref[rows_of, :]
        return turned.astype(jnp.bfloat16).astype(jnp.float32)

    for step in range(steps):
        rows_of = pl.ds(step * slots, slots)
        for at in range(local_heads):
            query_ref[:, step * local_heads + at, :] = turn(query_sum[rows_of, pl.ds(at * HD, HD)])

    for which in range(2):
        for at in range(pieces):
            pltpu.make_async_copy(parts.at[which, at], parts.at[which, at], kr.at[which, at]).wait()
    joined = [
        jnp.concatenate([parts[which, at] for at in range(pieces)], axis=1).astype(jnp.float32)
        for which in range(2)
    ]
    rows_of = slice(None)
    turned = turn(joined[0])
    for step in range(steps):
        new_keys[step] = turned[step * slots:(step + 1) * slots]
        new_values[step] = joined[1][step * slots:(step + 1) * slots]

    def own_of(slot):
        row = pl.ds(slot, 1)
        return [new_keys[i, row, :] for i in range(steps)], [new_values[i, row, :] for i in range(steps)]

    def cache_chunk(at, carry):
        for inner in range(chunk):
            slot = at * chunk + inner
            keys, values = own_of(slot)
            cache_out[slot] = attend(
                query_ref[slot], cache[0, slot], cache[1, slot], length_ref[slot], keys, values, local_heads)
        return carry

    groups = kv_heads
    each = chunks // groups
    for group in range(groups):
        if group + 1 < kv_heads:
            slot = slot_of(plane_of(group + 1), side, copy_of)
            arrive(slot, p1r.at[group + 1])
            spread(group + 1, prompts.at[slot], slot)
        pass_on(group)
        for at in range(group * each, (group + 1) * each):
            loads[at].wait()
        lax.fori_loop(group * each, (group + 1) * each, cache_chunk, 0)

    keep.wait()
    per_plane = share * 2 * per_device
    batch = min(8, per_plane)
    for group in range(kv_heads):
        plane = plane_of(group)
        for other in range(share):
            arrive(slot_of(plane, lax.rem(side + share - other, share), 1 - copy_of), p3r.at[other, group])

        def prompt_chunk(at, carry, plane=plane):
            for inner in range(batch):
                sender = plane * (share * 2) + at * (batch // per_device) + inner // per_device
                within = inner % per_device
                request = sender * per_device + within
                slot = local_ref[request]
                keys, values = own_of(slot)
                prompt_out[request] = attend(
                    query_ref[slot], prompts[sender, 0, within], prompts[sender, 1, within],
                    plength_ref[request], keys, values, local_heads)
            return carry

        lax.fori_loop(0, per_plane // batch, prompt_chunk, 0)

    def choose(slot, carry):
        cache_out[slot] = jnp.where(matched_ref[slot] > 0, prompt_out[request_ref[slot]], cache_out[slot])
        return carry

    lax.fori_loop(0, slots, choose, 0)
    for step in range(steps):
        for at in range(local_heads):
            heads_ref[pl.ds(step * slots, slots), pl.ds(at * HD, HD)] = cache_out[
                :, step * local_heads + at, :].astype(jnp.bfloat16)

    project_out(size, weights, heads_ref, out_ref, wbuf, own_sum, send1, recv1, send2, recv2, s1s, s1r, s2s, s2r)
    for copy in sent:
        copy.wait_send()
    for target, copy in part_copies:
        @pl.when(target != rank)
        def _(copy=copy):
            copy.wait_send()


def attention_block(
    lengths, plengths, local_slot, request, matched, gain, cosine, sine,
    hidden_in, w_query, w_keyval, cache_kv, prompt_kv, w_out, size,
):
    steps, slots, model_width = hidden_in.shape
    rows = steps * slots
    columns = w_query.shape[1]
    head_rows = steps * columns // HD
    width = w_keyval.shape[1]
    share = size // (prompt_kv.shape[3] // HD)
    kv_heads = prompt_kv.shape[3] // HD
    requests = plengths.shape[0]
    senders = requests // prompt_kv.shape[1]
    out_width = w_out.shape[1] // size
    half = size // 2
    splits = 8
    smem = pl.BlockSpec(memory_space=pltpu.SMEM)
    vmem = pl.BlockSpec(memory_space=pltpu.VMEM)
    hbm = pl.BlockSpec(memory_space=pl.ANY)
    dma = pltpu.SemaphoreType.DMA
    return pl.pallas_call(
        functools.partial(whole_kernel, size),
        out_shape=jax.ShapeDtypeStruct((rows, out_width), jnp.bfloat16),
        in_specs=[smem] * 5 + [vmem] * 3 + [hbm] * 6,
        out_specs=vmem,
        scratch_shapes=[
            pltpu.VMEM((rows, model_width), jnp.bfloat16),
            pltpu.VMEM(w_query.shape, jnp.bfloat16),
            pltpu.VMEM(w_keyval.shape, jnp.bfloat16),
            pltpu.VMEM((rows, columns), jnp.float32),
            pltpu.VMEM((rows, width), jnp.float32),
            pltpu.VMEM((rows, width), jnp.bfloat16),
            pltpu.VMEM((slots, head_rows, HD), jnp.float32),
            pltpu.VMEM((rows, columns), jnp.bfloat16),
            pltpu.VMEM(cache_kv.shape, jnp.bfloat16),
            pltpu.VMEM((senders, 2, prompt_kv.shape[1], prompt_kv.shape[2], HD), jnp.bfloat16),
            pltpu.VMEM((2, HD // width, rows, width), jnp.bfloat16),
            pltpu.VMEM((steps, slots, HD), jnp.float32),
            pltpu.VMEM((steps, slots, HD), jnp.float32),
            pltpu.VMEM((slots, head_rows, HD), jnp.float32),
            pltpu.VMEM((requests, head_rows, HD), jnp.float32),
            pltpu.VMEM((half, 2, columns, out_width), jnp.bfloat16),
            pltpu.VMEM((half, rows, out_width), jnp.float32),
            pltpu.VMEM((half, rows, out_width), jnp.bfloat16),
            pltpu.VMEM((half, rows, out_width), jnp.bfloat16),
            pltpu.VMEM((half - 1, rows, out_width), jnp.bfloat16),
            pltpu.VMEM((half - 1, rows, out_width), jnp.bfloat16),
            dma((steps,)), dma((splits,)), dma((splits,)),
            dma((slots // 8,)),
            dma,
            dma((kv_heads,)), dma((kv_heads,)),
            dma((share, kv_heads)), dma((share, kv_heads)),
            dma((share, kv_heads)), dma((share, kv_heads)),
            dma((share,)), dma((2, HD // width)),
            dma((half, 2)), dma((half,)), dma((half,)), dma((half - 1,)), dma((half - 1,)),
        ],
        compiler_params=pltpu.CompilerParams(collective_id=1, has_side_effects=True, vmem_limit_bytes=56 * 2**20),
    )(lengths, plengths, local_slot, request, matched, gain, cosine, sine,
      hidden_in, w_query, w_keyval, cache_kv, prompt_kv, w_out)


def local(
    hidden_in,
    norm_gain,
    w_query,
    w_keyval,
    w_out,
    cache_kv,
    cache_len,
    prompt_kv,
    block_count,
    slot_of,
):
    tensor_size = lax.axis_size("tensor")
    replica_rank = lax.axis_index("replica")
    step_count, row_count, model_width = hidden_in.shape
    slot_ids = replica_rank * row_count + jnp.arange(row_count, dtype=jnp.int32)
    matches = slot_of[None, :] == slot_ids[:, None]
    matched = jnp.any(matches, 1)
    request_count = slot_of.shape[0]
    request = jnp.sum(jnp.where(matches, jnp.arange(request_count, dtype=jnp.int32)[None, :], 0), 1)
    prompt_len = jnp.sum(jnp.where(matches, block_count[None, :], 0), 1) * BLOCK
    base_pos = jnp.where(matched, prompt_len, cache_len)
    positions = base_pos[None, :] + jnp.arange(step_count, dtype=jnp.int32)[:, None]
    half_dim = HD // 2
    freqs = THETA ** (-2.0 * jnp.arange(half_dim, dtype=jnp.float32) / HD)
    angles = positions[..., None].astype(jnp.float32) * freqs
    cosine = jnp.cos(angles)
    sine = jnp.sin(angles)
    cosine = jnp.concatenate([cosine, cosine], -1)
    sine = jnp.concatenate([-sine, sine], -1)
    local_slot = jnp.clip(slot_of - replica_rank * row_count, 0, row_count - 1)
    mixed = attention_block(
        cache_len,
        block_count * BLOCK,
        local_slot,
        request,
        matched.astype(jnp.int32),
        norm_gain.astype(jnp.float32)[None, :],
        cosine.reshape(step_count * row_count, HD),
        sine.reshape(step_count * row_count, HD),
        hidden_in,
        w_query,
        w_keyval,
        cache_kv,
        prompt_kv,
        w_out,
        tensor_size,
    )
    return mixed.reshape(step_count, row_count, -1)


def solution(mesh):
    in_specs = (
        P(None, ("group", "replica"), None),
        P(),
        P(None, "tensor"),
        P(None, "tensor"),
        P("tensor", None),
        P(None, ("group", "replica"), None, "tensor"),
        P(("group", "replica")),
        P(None, ("group", "tensor", "replica"), None, None),
        P("group"),
        P("group"),
    )
    out_specs = P(None, ("group", "replica"), "tensor")
    return jax.shard_map(local, mesh=mesh, in_specs=in_specs, out_specs=out_specs, check_vma=False)
```

```python
import functools

import jax
import jax.numpy as jnp
from jax import lax
from jax.experimental import pallas as pl
from jax.experimental.pallas import tpu as pltpu
from jax.sharding import PartitionSpec as P

KVH = 4
HD = 128
GROUP = 8
BLOCK = 64


EPSILON = 1e-05
THETA = 500000.0
NEGATIVE = -1e30
MESH = pl.DeviceIdType.MESH


def load_out(size, w_ref, wbuf, wsem, width):
    half = size // 2
    rank = lax.axis_index("tensor")
    mine = rank // 2
    side = lax.rem(rank, 2)
    offsets = [o for o in range(half // 2, half)] + [o for o in range(1, half // 2)] + [0]

    weights = []
    for at, off in enumerate(offsets):
        block = lax.rem(mine + off, half)
        for which, target in enumerate((2 * block + 1 - side, 2 * block + side)):
            columns = pl.ds(pl.multiple_of(target * width, 128), width)
            copy = pltpu.make_async_copy(w_ref.at[:, columns], wbuf.at[at, which], wsem.at[at, which])
            copy.start()
            weights.append(copy)
    return weights


def project_out(size, weights, heads_ref, out_ref, wbuf, own, send1, recv1, send2, recv2, s1s, s1r, s2s, s2r):
    half = size // 2
    rank = lax.axis_index("tensor")
    mine = rank // 2
    side = lax.rem(rank, 2)
    partner = rank + 1 - 2 * side
    offsets = [o for o in range(half // 2, half)] + [o for o in range(1, half // 2)] + [0]

    heads = heads_ref[...]
    first = []
    for at in range(half):
        weights[2 * at].wait()
        send1[at] = jnp.dot(heads, wbuf[at, 0], preferred_element_type=jnp.float32).astype(jnp.bfloat16)
        copy = pltpu.make_async_remote_copy(
            src_ref=send1.at[at], dst_ref=recv1.at[at], send_sem=s1s.at[at], recv_sem=s1r.at[at],
            device_id={"tensor": partner}, device_id_type=MESH)
        copy.start()
        first.append(copy)
    for at in range(half):
        weights[2 * at + 1].wait()
        own[at] = jnp.dot(heads, wbuf[at, 1], preferred_element_type=jnp.float32)
    second = []
    for at, off in enumerate(offsets):
        first[at].wait_recv()
        total = own[at] + recv1[at].astype(jnp.float32)
        if off != 0:
            send2[at] = total.astype(jnp.bfloat16)
            copy = pltpu.make_async_remote_copy(
                src_ref=send2.at[at], dst_ref=recv2.at[at], send_sem=s2s.at[at], recv_sem=s2r.at[at],
                device_id={"tensor": 2 * lax.rem(mine + off, half) + side}, device_id_type=MESH)
            copy.start()
            second.append(copy)
        else:
            own[at] = total
    for at in range(half - 1):
        second[at].wait_recv()
        own[half - 1] += recv2[at].astype(jnp.float32)
    out_ref[...] = own[half - 1].astype(jnp.bfloat16)
    for copy in first + second:
        copy.wait_send()


def attend(query, keys, values, length, own_keys, own_values, local_heads):
    scaling = HD ** (-0.5)
    score = lax.dot_general(
        query.astype(jnp.bfloat16), keys, (((1,), (1,)), ((), ())), preferred_element_type=jnp.float32
    ) * scaling
    score = jnp.where(lax.broadcasted_iota(jnp.int32, score.shape, 1) < length, score, NEGATIVE)
    step_of = lax.broadcasted_iota(jnp.int32, (query.shape[0], 1), 0) // local_heads
    own = []
    for step, key in enumerate(own_keys):
        one = jnp.sum(query * key, axis=1, keepdims=True) * scaling
        own.append(jnp.where(step_of >= step, one, NEGATIVE))
    top = jnp.max(score, axis=1, keepdims=True)
    for one in own:
        top = jnp.maximum(top, one)
    score = jnp.exp(score - top)
    own = [jnp.exp(one - top) for one in own]
    summed = jnp.sum(score, axis=1, keepdims=True)
    for one in own:
        summed = summed + one
    inverse = 1.0 / summed
    result = jnp.dot((score * inverse).astype(jnp.bfloat16), values, preferred_element_type=jnp.float32)
    for one, value in zip(own, own_values):
        result = result + (one * inverse).astype(jnp.bfloat16).astype(jnp.float32) * value
    return result


def whole_kernel(
    size, length_ref, plength_ref, local_ref, request_ref, matched_ref,
    gain_ref, cosine_ref, sine_ref, hidden_ref, wq_ref, wkv_ref, cache_ref, prompt_ref, w_ref, out_ref,
    normed, wq, wkv, query_sum, part_sum, part_ref, query_ref, heads_ref,
    cache, prompts, parts, new_keys, new_values, cache_out, prompt_out,
    wbuf, own_sum, send1, recv1, send2, recv2,
    hsem, qsem, vsem, csem, lsem, p1s, p1r, p2s, p2r, p3s, p3r, ks, kr, wsem, s1s, s1r, s2s, s2r,
):
    slots, head_rows, _ = query_ref.shape
    depth = wq.shape[0] // qsem.shape[0]
    steps = new_keys.shape[0]
    local_heads = head_rows // steps
    kv_heads = prompt_ref.shape[3] // HD
    per_device = prompt_ref.shape[1]
    share = size // kv_heads
    pieces = parts.shape[1]
    rank = lax.axis_index("tensor")
    copy_of = lax.axis_index("replica")
    head = rank // share
    side = lax.rem(rank, share)
    offsets = [0] + list(range(kv_heads // 2, kv_heads)) + list(range(1, kv_heads // 2))
    chunk = 8

    hidden_loads = []
    for step in range(steps):
        copy = pltpu.make_async_copy(hidden_ref.at[step], normed.at[pl.ds(step * slots, slots)], hsem.at[step])
        copy.start()
        hidden_loads.append(copy)

    def weight_loads(at):
        deep = pl.ds(pl.multiple_of(at * depth, depth), depth)
        return (
            pltpu.make_async_copy(wq_ref.at[deep], wq.at[deep], qsem.at[at]),
            pltpu.make_async_copy(wkv_ref.at[deep], wkv.at[deep], vsem.at[at]),
        )

    for at in range(qsem.shape[0]):
        for copy in weight_loads(at):
            copy.start()

    barrier = pltpu.get_barrier_semaphore()
    for off in range(1, size):
        pl.semaphore_signal(barrier, inc=1, device_id={"tensor": lax.rem(rank + off, size)}, device_id_type=MESH)
    pl.semaphore_signal(barrier, inc=1, device_id={"replica": 1 - copy_of}, device_id_type=MESH)
    pl.semaphore_wait(barrier, size)

    def slot_of(plane, side_at, replica_at):
        return (plane * share + side_at) * 2 + replica_at

    def arrive(slot, which, sem):
        pltpu.make_async_copy(prompts.at[slot, which], prompts.at[slot, which], sem).wait()

    sent = []

    def send(src, slot, which, send_sem, recv_sem, device):
        copy = pltpu.make_async_remote_copy(
            src_ref=src, dst_ref=prompts.at[slot, which], send_sem=send_sem, recv_sem=recv_sem,
            device_id=device, device_id_type=MESH)
        copy.start()
        return copy

    def plane_of(at):
        return lax.rem(head + kv_heads - offsets[at], kv_heads)

    def slab(plane, which):
        return prompt_ref.at[which, :, :, pl.ds(pl.multiple_of(plane * HD, HD), HD)]

    mine = slot_of(head, side, copy_of)
    turns = [(at, which) for at in range(1, kv_heads) for which in range(2)]
    outgoing = []

    def send_next():
        if len(outgoing) < len(turns):
            at, which = turns[len(outgoing)]
            target = lax.rem(head + offsets[at], kv_heads)
            outgoing.append(send(
                slab(target, which), mine, which, p1s.at[at, which], p1r.at[at, which],
                {"tensor": target * share + side}))

    def spread(at, which, src, slot):
        for other in range(1, share):
            target = head * share + lax.rem(side + other, share)
            sent.append(send(
                src, slot, which, p2s.at[other, at, which], p2r.at[other, at, which], {"tensor": target}))
        sent.append(send(src, slot, which, p3s.at[0, at, which], p3r.at[0, at, which], {"replica": 1 - copy_of}))

    def pass_on(at, which):
        for other in range(1, share):
            slot = slot_of(plane_of(at), lax.rem(side + share - other, share), copy_of)
            arrive(slot, which, p2r.at[other, at, which])
            sent.append(send(
                prompts.at[slot, which], slot, which, p3s.at[other, at, which], p3r.at[other, at, which],
                {"replica": 1 - copy_of}))

    send_next()
    send_next()
    for which in range(2):
        spread(0, which, slab(head, which), mine)
    keeps = [pltpu.make_async_copy(slab(head, which), prompts.at[mine, which], lsem.at[which]) for which in range(2)]
    for keep in keeps:
        keep.start()

    loads = []
    chunks = slots // chunk
    for at in range(chunks):
        rows = pl.ds(at * chunk, chunk)
        copy = pltpu.make_async_copy(cache_ref.at[:, rows], cache.at[:, rows], csem.at[at])
        copy.start()
        loads.append(copy)
    weights = load_out(size, w_ref, wbuf, wsem, out_ref.shape[1])

    for copy in hidden_loads:
        copy.wait()

    def normalize(at, carry):
        rows = pl.ds(pl.multiple_of(at * 16, 16), 16)
        hidden = normed[rows, :].astype(jnp.float32)
        scale = lax.rsqrt(jnp.mean(hidden * hidden, axis=1, keepdims=True) + EPSILON)
        normed[rows, :] = (hidden * scale * gain_ref[...]).astype(jnp.bfloat16)
        return carry

    lax.fori_loop(0, normed.shape[0] // 16, normalize, 0)
    query_sum[...] = jnp.zeros_like(query_sum)
    part_sum[...] = jnp.zeros_like(part_sum)

    def project_in(at, carry):
        for copy in weight_loads(at):
            copy.wait()
        deep = pl.ds(pl.multiple_of(at * depth, depth), depth)
        part = normed[:, deep]
        query_sum[...] += jnp.dot(part, wq[deep, :], preferred_element_type=jnp.float32)
        part_sum[...] += jnp.dot(part, wkv[deep, :], preferred_element_type=jnp.float32)
        return carry

    lax.fori_loop(0, qsem.shape[0], project_in, 0)
    part_ref[...] = part_sum[...].astype(jnp.bfloat16)

    column = rank // pieces
    kind = column // kv_heads
    piece = lax.rem(rank, pieces)
    part_copies = []
    for at in range(share):
        target = lax.rem(column, kv_heads) * share + at
        remote = pltpu.make_async_remote_copy(
            src_ref=part_ref, dst_ref=parts.at[kind, piece], send_sem=ks.at[at], recv_sem=kr.at[kind, piece],
            device_id={"tensor": target}, device_id_type=MESH)
        part_copies.append((target, remote))

        @pl.when(target != rank)
        def _(remote=remote):
            remote.start()

        @pl.when(target == rank)
        def _():
            pltpu.make_async_copy(part_ref, parts.at[kind, piece], kr.at[kind, piece]).start()

    def turn(values):
        turned = values * cosine_ref[rows_of, :] + pltpu.roll(values, HD // 2, 1) * sine_ref[rows_of, :]
        return turned.astype(jnp.bfloat16).astype(jnp.float32)

    for step in range(steps):
        rows_of = pl.ds(step * slots, slots)
        for at in range(local_heads):
            query_ref[:, step * local_heads + at, :] = turn(query_sum[rows_of, pl.ds(at * HD, HD)])

    for which in range(2):
        for at in range(pieces):
            pltpu.make_async_copy(parts.at[which, at], parts.at[which, at], kr.at[which, at]).wait()
    joined = [
        jnp.concatenate([parts[which, at] for at in range(pieces)], axis=1).astype(jnp.float32)
        for which in range(2)
    ]
    rows_of = slice(None)
    turned = turn(joined[0])
    for step in range(steps):
        new_keys[step] = turned[step * slots:(step + 1) * slots]
        new_values[step] = joined[1][step * slots:(step + 1) * slots]

    def own_of(slot):
        row = pl.ds(slot, 1)
        return [new_keys[i, row, :] for i in range(steps)], [new_values[i, row, :] for i in range(steps)]

    def cache_chunk(at, carry):
        for inner in range(chunk):
            slot = at * chunk + inner
            keys, values = own_of(slot)
            cache_out[slot] = attend(
                query_ref[slot], cache[0, slot], cache[1, slot], length_ref[slot], keys, values, local_heads)
        return carry

    per_plane = share * 2 * per_device
    batch = min(8, per_plane)

    def prompt_plane(at):
        plane = plane_of(at)
        for which in range(2):
            for other in range(share):
                slot = slot_of(plane, lax.rem(side + share - other, share), 1 - copy_of)
                arrive(slot, which, p3r.at[other, at, which])

        def prompt_chunk(step, carry):
            for inner in range(batch):
                sender = plane * (share * 2) + step * (batch // per_device) + inner // per_device
                within = inner % per_device
                request = sender * per_device + within
                slot = local_ref[request]
                keys, values = own_of(slot)
                prompt_out[request] = attend(
                    query_ref[slot], prompts[sender, 0, within], prompts[sender, 1, within],
                    plength_ref[request], keys, values, local_heads)
            return carry

        lax.fori_loop(0, per_plane // batch, prompt_chunk, 0)

    waiting = [(0, 0), (0, 1)]
    done = 0
    for step, (at, which) in enumerate(turns):
        slot = slot_of(plane_of(at), side, copy_of)
        arrive(slot, which, p1r.at[at, which])
        outgoing[step].wait_send()
        send_next()
        spread(at, which, prompts.at[slot, which], slot)
        if step == 0:
            pass_on(*waiting.pop(0))
        pass_on(*waiting.pop(0))
        waiting.append((at, which))
        upto = min(chunks, -(-chunks * (step + 1) // len(turns)))
        for number in range(done, upto):
            loads[number].wait()
        lax.fori_loop(done, upto, cache_chunk, 0)
        done = upto
        if which == 1:
            if at == 1:
                for keep in keeps:
                    keep.wait()
            prompt_plane(at - 1)
    for late in waiting:
        pass_on(*late)
    prompt_plane(kv_heads - 1)

    def choose(slot, carry):
        cache_out[slot] = jnp.where(matched_ref[slot] > 0, prompt_out[request_ref[slot]], cache_out[slot])
        return carry

    lax.fori_loop(0, slots, choose, 0)
    for step in range(steps):
        for at in range(local_heads):
            heads_ref[pl.ds(step * slots, slots), pl.ds(at * HD, HD)] = cache_out[
                :, step * local_heads + at, :].astype(jnp.bfloat16)

    project_out(size, weights, heads_ref, out_ref, wbuf, own_sum, send1, recv1, send2, recv2, s1s, s1r, s2s, s2r)
    for copy in sent:
        copy.wait_send()
    for target, copy in part_copies:
        @pl.when(target != rank)
        def _(copy=copy):
            copy.wait_send()


def attention_block(
    lengths, plengths, local_slot, request, matched, gain, cosine, sine,
    hidden_in, w_query, w_keyval, cache_kv, prompt_kv, w_out, size,
):
    steps, slots, model_width = hidden_in.shape
    rows = steps * slots
    columns = w_query.shape[1]
    head_rows = steps * columns // HD
    width = w_keyval.shape[1]
    share = size // (prompt_kv.shape[3] // HD)
    kv_heads = prompt_kv.shape[3] // HD
    requests = plengths.shape[0]
    senders = requests // prompt_kv.shape[1]
    out_width = w_out.shape[1] // size
    half = size // 2
    splits = 8
    smem = pl.BlockSpec(memory_space=pltpu.SMEM)
    vmem = pl.BlockSpec(memory_space=pltpu.VMEM)
    hbm = pl.BlockSpec(memory_space=pl.ANY)
    dma = pltpu.SemaphoreType.DMA
    return pl.pallas_call(
        functools.partial(whole_kernel, size),
        out_shape=jax.ShapeDtypeStruct((rows, out_width), jnp.bfloat16),
        in_specs=[smem] * 5 + [vmem] * 3 + [hbm] * 6,
        out_specs=vmem,
        scratch_shapes=[
            pltpu.VMEM((rows, model_width), jnp.bfloat16),
            pltpu.VMEM(w_query.shape, jnp.bfloat16),
            pltpu.VMEM(w_keyval.shape, jnp.bfloat16),
            pltpu.VMEM((rows, columns), jnp.float32),
            pltpu.VMEM((rows, width), jnp.float32),
            pltpu.VMEM((rows, width), jnp.bfloat16),
            pltpu.VMEM((slots, head_rows, HD), jnp.float32),
            pltpu.VMEM((rows, columns), jnp.bfloat16),
            pltpu.VMEM(cache_kv.shape, jnp.bfloat16),
            pltpu.VMEM((senders, 2, prompt_kv.shape[1], prompt_kv.shape[2], HD), jnp.bfloat16),
            pltpu.VMEM((2, HD // width, rows, width), jnp.bfloat16),
            pltpu.VMEM((steps, slots, HD), jnp.float32),
            pltpu.VMEM((steps, slots, HD), jnp.float32),
            pltpu.VMEM((slots, head_rows, HD), jnp.float32),
            pltpu.VMEM((requests, head_rows, HD), jnp.float32),
            pltpu.VMEM((half, 2, columns, out_width), jnp.bfloat16),
            pltpu.VMEM((half, rows, out_width), jnp.float32),
            pltpu.VMEM((half, rows, out_width), jnp.bfloat16),
            pltpu.VMEM((half, rows, out_width), jnp.bfloat16),
            pltpu.VMEM((half - 1, rows, out_width), jnp.bfloat16),
            pltpu.VMEM((half - 1, rows, out_width), jnp.bfloat16),
            dma((steps,)), dma((splits,)), dma((splits,)),
            dma((slots // 8,)),
            dma((2,)),
            dma((kv_heads, 2)), dma((kv_heads, 2)),
            dma((share, kv_heads, 2)), dma((share, kv_heads, 2)),
            dma((share, kv_heads, 2)), dma((share, kv_heads, 2)),
            dma((share,)), dma((2, HD // width)),
            dma((half, 2)), dma((half,)), dma((half,)), dma((half - 1,)), dma((half - 1,)),
        ],
        compiler_params=pltpu.CompilerParams(collective_id=1, has_side_effects=True, vmem_limit_bytes=56 * 2**20),
    )(lengths, plengths, local_slot, request, matched, gain, cosine, sine,
      hidden_in, w_query, w_keyval, cache_kv, prompt_kv, w_out)


def local(
    hidden_in,
    norm_gain,
    w_query,
    w_keyval,
    w_out,
    cache_kv,
    cache_len,
    prompt_kv,
    block_count,
    slot_of,
):
    tensor_size = lax.axis_size("tensor")
    replica_rank = lax.axis_index("replica")
    step_count, row_count, model_width = hidden_in.shape
    slot_ids = replica_rank * row_count + jnp.arange(row_count, dtype=jnp.int32)
    matches = slot_of[None, :] == slot_ids[:, None]
    matched = jnp.any(matches, 1)
    request_count = slot_of.shape[0]
    request = jnp.sum(jnp.where(matches, jnp.arange(request_count, dtype=jnp.int32)[None, :], 0), 1)
    prompt_len = jnp.sum(jnp.where(matches, block_count[None, :], 0), 1) * BLOCK
    base_pos = jnp.where(matched, prompt_len, cache_len)
    positions = base_pos[None, :] + jnp.arange(step_count, dtype=jnp.int32)[:, None]
    half_dim = HD // 2
    freqs = THETA ** (-2.0 * jnp.arange(half_dim, dtype=jnp.float32) / HD)
    angles = positions[..., None].astype(jnp.float32) * freqs
    cosine = jnp.cos(angles)
    sine = jnp.sin(angles)
    cosine = jnp.concatenate([cosine, cosine], -1)
    sine = jnp.concatenate([-sine, sine], -1)
    local_slot = jnp.clip(slot_of - replica_rank * row_count, 0, row_count - 1)
    mixed = attention_block(
        cache_len,
        block_count * BLOCK,
        local_slot,
        request,
        matched.astype(jnp.int32),
        norm_gain.astype(jnp.float32)[None, :],
        cosine.reshape(step_count * row_count, HD),
        sine.reshape(step_count * row_count, HD),
        hidden_in,
        w_query,
        w_keyval,
        cache_kv,
        prompt_kv,
        w_out,
        tensor_size,
    )
    return mixed.reshape(step_count, row_count, -1)


def solution(mesh):
    in_specs = (
        P(None, ("group", "replica"), None),
        P(),
        P(None, "tensor"),
        P(None, "tensor"),
        P("tensor", None),
        P(None, ("group", "replica"), None, "tensor"),
        P(("group", "replica")),
        P(None, ("group", "tensor", "replica"), None, None),
        P("group"),
        P("group"),
    )
    out_specs = P(None, ("group", "replica"), "tensor")
    return jax.shard_map(local, mesh=mesh, in_specs=in_specs, out_specs=out_specs, check_vma=False)
```
